32 devices in a mesh: row: 2 (over core), col: 16 (over z, y, x).
Axes of the slice: x: 2, y: 2, z: 4, core: 2. Of those that a mesh axis runs over, the one named last changes fastest.
Arguments:
- panel_adj: float32 [14336, 512], P('row', 'col'), may hold values from -6 to 6
- inv_diag: float32 [512, 512], P('col'), may hold values from -0.25 to 0.25
- row_panel: float32 [512, 14336], P('row', 'col'), may hold values from -0.25 to 0.25
- trailing_adj: float32 [14336, 14336], P('row', 'col'), may hold values from -6 to 6
- trailing_factor: float32 [14336, 14336], P('row', 'col'), may hold values from -0.046875 to 0.046875
Outputs:
- trailing_new: float32 [14336, 14336], P('row', 'col')
- row_adj: float32 [512, 14336], P('row', 'col')
The draws below stay inside these ranges and needn't reach their ends.
All inputs are finite; a program needn't handle non-finite values.
Results may differ from the reference program's by a relative error of at most 0.00007.
Values sent between devices are 32-bit elements; how exact they have to be, the bound alone decides.
No kernel may reach another device: no remote copies, remote signals or barrier semaphores. Data moves between devices by JAX's collectives and lax.ppermute only.
A program may use at most 192 MiB of HBM per device.

```python
import jax
import jax.numpy as jnp
from jax import lax

NB = 512
M = 14336


def block_scale(own_key, dims, pieces, least, high):
    def one(dim, blocks):
        heights = jax.random.uniform(jax.random.fold_in(jax.random.fold_in(own_key, 6), dim), (blocks,), jnp.float32, least / len(pieces), high / len(pieces))
        return jnp.repeat(jnp.exp(heights), dims[dim] // blocks).reshape((-1,) + (1,) * (len(dims) - dim - 1))

    factor_of = one(*pieces[0])
    for cut in pieces[1:]:
        factor_of = factor_of * one(*cut)
    return factor_of


def gaussian(key, dims, scale, reach, cuts=(), dtype=jnp.bfloat16):
    entries = jax.random.normal(key, dims, jnp.float32) * scale
    if len(cuts) > 0:
        entries = block_scale(key, dims, cuts, -0.22, 0.18) * entries
    return jnp.clip(entries, min=-reach, max=reach).astype(dtype)


def setup_inputs(seed: int = 0) -> dict:
    keys = jax.random.split(jax.random.key(seed), 6)
    panel_adj = gaussian(keys[0], (M, NB), 1.0, 6.0, ((0, 2), (1, 16)), jnp.float32)
    inv_diag = gaussian(keys[1], (NB, NB), NB ** -0.5, 0.25, ((0, 16),), jnp.float32)
    row_panel = gaussian(keys[2], (NB, M), NB ** -0.5, 0.25, ((0, 2), (1, 16)), jnp.float32)
    trailing_adj = gaussian(keys[3], (M, M), 1.0, 6.0, ((0, 2), (1, 16)), jnp.float32)
    trailing_factor = gaussian(keys[4], (M, M), M ** -0.5, 0.046875, ((0, 2), (1, 16)), jnp.float32)
    return dict(panel_adj=panel_adj, inv_diag=inv_diag, row_panel=row_panel, trailing_adj=trailing_adj, trailing_factor=trailing_factor)


def reference(panel_adj, inv_diag, row_panel, trailing_adj, trailing_factor):
    highest = lax.Precision.HIGHEST
    scaled = jnp.dot(panel_adj, inv_diag, precision=highest, preferred_element_type=jnp.float32)
    trailing_new = trailing_adj - jnp.dot(scaled, row_panel, precision=highest, preferred_element_type=jnp.float32)
    row_adj = lax.dot_general(scaled, trailing_factor, (((0,), (0,)), ((), ())), precision=highest, preferred_element_type=jnp.float32)
    return trailing_new, row_adj
```

```python
import functools

import jax
import jax.numpy as jnp
from jax import lax
from jax.experimental import pallas as pl
from jax.experimental.pallas import tpu as pltpu
from jax.sharding import PartitionSpec as P

F32, BF16 = jnp.float32, jnp.bfloat16
VMEM_BYTES = 32 << 20
HIGHEST = lax.Precision.HIGHEST


def two_terms(x):
    high = x.astype(BF16)
    return high, (x - high.astype(F32)).astype(BF16)


def dot(a, b, dims=(((1,), (0,)), ((), ()))):
    return lax.dot_general(a, b, dims, preferred_element_type=F32)


def dot3(a, b, dims=(((1,), (0,)), ((), ()))):
    return dot(a[0], b[0], dims) + dot(a[0], b[1], dims) + dot(a[1], b[0], dims)


def panel_kernel(places, first, *refs):
    n = len(places)
    pieces, (factor, adj, w), refs = refs[:n], refs[n : n + 3], refs[n + 3 :]
    if not first:
        refs = refs[2:]
    out, sums, p_high, p_low, w_high, w_low = refs

    @pl.when(pl.program_id(0) == 0)
    def _():
        if first:
            sums[...] = jnp.zeros_like(sums)
        w_high[...], w_low[...] = two_terms(w[...])

    for piece, place in zip(pieces, places):
        high, low = two_terms(piece[...])
        for src, rows, dst in place:
            p_high[dst : dst + rows, :] = high[src : src + rows]
            p_low[dst : dst + rows, :] = low[src : src + rows]
    panel = p_high[...], p_low[...]
    sums[...] += dot3(panel, two_terms(factor[...]))
    out[...] = adj[...] - dot3(panel, (w_high[...], w_low[...]), (((0,), (0,)), ((), ())))


def panel_step(early, pieces, places, factor, adj, w, state, start, skip, size, tile):
    rows, cols = factor.shape
    depth = w.shape[0]
    at, off = start // tile, skip // tile
    held = pl.BlockSpec(memory_space=pltpu.VMEM)
    tiled = pl.BlockSpec((tile, cols), lambda i: (i + at, 0))
    n = len(early) + len(pieces)
    first = state is None
    args = [*early, *pieces, factor, adj, w]
    in_specs = [pl.BlockSpec((p.shape[0], tile), lambda i: (0, i + at)) for p in early]
    in_specs += [pl.BlockSpec((p.shape[0], tile), lambda i: (0, i + off)) for p in pieces] + [tiled, tiled, held]
    aliases = {}
    if not first:
        args += [state[1], state[0]]
        in_specs += [held, pl.BlockSpec(memory_space=pl.ANY)]
        aliases = {n + 3: 1, n + 4: 0}
    return pl.pallas_call(
        functools.partial(panel_kernel, places, first),
        grid=(size // tile,),
        in_specs=in_specs,
        out_specs=[tiled, held],
        out_shape=[jax.ShapeDtypeStruct((rows, cols), F32), pltpu.VMEM((depth, cols), F32)],
        input_output_aliases=aliases,
        scratch_shapes=[pltpu.VMEM((depth, tile), BF16)] * 2 + [pltpu.VMEM((depth, cols), BF16)] * 2,
        compiler_params=pltpu.CompilerParams(vmem_limit_bytes=VMEM_BYTES),
        cost_estimate=pl.CostEstimate(
            flops=18 * size * depth * cols, bytes_accessed=12 * size * cols, transcendentals=0
        ),
    )(*args)


def cut(rows):
    tile = 256
    while rows % tile or rows // tile < 14:
        tile //= 2
    tiles = rows // tile
    part = tiles // 14
    sizes = [part, 4 * part, 4 * part, tiles - 11 * part, 2 * part]
    return [s * tile for s in sizes], tile


def after(x, *done):
    return lax.optimization_barrier((x, *done))[0] if done else x


def local(panel_adj, inv_diag, row_panel, trailing_adj, trailing_factor):
    n_row, n_col = lax.axis_size("row"), lax.axis_size("col")
    rows, kb = panel_adj.shape
    depth = kb * n_col
    planes = n_col // 4
    pairs = dict(
        x=[(c, c ^ 1) for c in range(n_col)],
        y=[(c, c ^ 2) for c in range(n_col)],
        up=[(c, (c + 4) % n_col) for c in range(n_col)],
        down=[(c, (c - 4) % n_col) for c in range(n_col)],
    )

    def send(way, x, *done):
        return lax.ppermute(after(x, *done), "col", pairs[way])

    def over_row(x, *done):
        if n_row == 2:
            return x + lax.ppermute(after(x, *done), "row", [(0, 1), (1, 0)])
        return lax.psum(x, "row")

    def cross(block, *done):
        block = after(block, *done)
        return send("x", block), send("y", block)

    def corner(x, y, *done):
        x, y = lax.optimization_barrier((x, y, *done))[:2]
        half = x.shape[0] // 2
        return send("x", y[:half]), send("y", x[half:])

    def along_z(block, *done):
        block = after(block, *done)
        return [block] + [
            lax.ppermute(block, "col", [(c, (c + 4 * j) % n_col) for c in range(n_col)]) for j in range(1, planes)
        ]

    own = panel_adj.T
    share = depth // n_row
    inv_own = lax.dynamic_slice(inv_diag, (0, lax.axis_index("row") * share), (kb, share))
    sizes, tile = cut(rows)
    starts = [sum(sizes[:i]) for i in range(len(sizes))]
    chunk = [own[:, a : a + n] for a, n in zip(starts, sizes)]
    n1 = sizes[0]
    chunk[0] = jnp.concatenate([chunk[0], inv_own], 1)
    wide1 = chunk[0].shape[1]

    def near(block, *done):
        return send("up", block, *done), send("down", block, *done)

    def far(block, up, down, *done):
        got = [block, up]
        while len(got) < planes - 1:
            got.append(send("up", got[-1], *done))
        return [*got, down]

    early = jnp.concatenate([chunk[0], chunk[4]], 1)
    z1 = along_z(chunk[0])
    x0, y0 = cross(early)
    xy0 = corner(x0, y0)
    z2 = along_z(chunk[1], x0, y0, *z1)
    rest1 = jnp.concatenate(z1[1:], 0)
    x1, y1 = cross(rest1, *xy0)
    d2 = jnp.concatenate(z2, 0)
    xy1 = corner(x1, y1)
    x2, y2 = cross(d2, x1, y1)
    z3 = along_z(chunk[2], *xy1)

    wide = kb * planes
    hk, hw, hr = kb // 2, wide // 2, (wide - kb) // 2
    z_places = [[(0, wide, 0)], [(0, wide, wide)], [(0, wide, 2 * wide)], [(0, hw, 3 * wide)], [(0, hw, 3 * wide + hw)]]
    p_places = [[(kb * q, kb, wide * q + kb * j) for q in range(4)] for j in range(planes)]
    first_places = [[(0, kb, 0)], [(0, kb, wide)], [(0, kb, 2 * wide)], [(0, hk, 3 * wide)], [(0, hk, 3 * wide + hk)],
                    [(0, wide - kb, kb)], [(0, wide - kb, wide + kb)], [(0, wide - kb, 2 * wide + kb)],
                    [(0, hr, 3 * wide + kb)], [(0, hr, 3 * wide + kb + hr)]]
    first = [p[:, :wide1] for p in (early, x0, y0, *xy0)] + [rest1, x1, y1, *xy1]
    inverse = jnp.concatenate([first[i][:, n1:] for i in (0, 5, 1, 6, 2, 7, 3, 4, 8, 9)], 0)
    w = over_row(jnp.dot(inverse, row_panel, precision=HIGHEST, preferred_element_type=F32))
    step = functools.partial(panel_step, [], factor=trailing_factor, adj=trailing_adj, w=w, tile=tile)

    def halves(got, state, c):
        size = sizes[c] // (2 * tile) * tile
        half = step(got, z_places, state=state, start=starts[c], skip=0, size=size)
        rest = sizes[c] - size
        return half, step(got, z_places, state=half, start=starts[c] + size, skip=size, size=rest)

    s1 = step(first, first_places, state=None, start=starts[0], skip=0, size=sizes[0])
    xy2 = corner(x2, y2, s1[1])
    d3 = jnp.concatenate(z3, 0)
    x3, y3 = cross(d3, x2, y2, s1[1])
    z4 = along_z(chunk[3], *xy2)
    s2a, s2 = halves([d2, x2, y2, *xy2], s1, 1)
    xy3 = corner(x3, y3, s2a[1])
    d4 = jnp.concatenate(z4, 0)
    x4, y4 = cross(d4, x3, y3, s2a[1])
    plane = jnp.concatenate([p[:, wide1:] for p in (early, x0, y0, *xy0)], 0)
    z5 = near(plane, z4[2], s2a[1])
    s3a, s3 = halves([d3, x3, y3, *xy3], s2, 2)
    xy4 = corner(x4, y4, s3a[1])
    z5 = far(plane, *z5, s3a[1])
    s5 = step(z5, p_places, state=s3, start=starts[4], skip=0, size=sizes[4])
    out, sums = step([d4, x4, y4, *xy4], z_places, state=s5, start=starts[3], skip=0, size=sizes[3])
    row_adj = lax.dot_general(
        inverse, over_row(sums), (((0,), (0,)), ((), ())), precision=HIGHEST, preferred_element_type=F32
    )
    return out, row_adj


def solution(mesh):
    placed = (P("row", "col"), P("col", None), P("row", "col"), P("row", "col"), P("row", "col"))
    return jax.shard_map(
        local,
        mesh=mesh,
        in_specs=placed,
        out_specs=(P("row", "col"), P("row", "col")),
        check_vma=False,
    )
```

```python
import functools

import jax
import jax.numpy as jnp
from jax import lax
from jax.experimental import pallas as pl
from jax.experimental.pallas import tpu as pltpu
from jax.sharding import PartitionSpec as P

F32, BF16 = jnp.float32, jnp.bfloat16
VMEM_BYTES = 32 << 20
HIGH = lax.Precision.HIGH


def two_terms(x):
    high = x.astype(BF16)
    return high, (x - high.astype(F32)).astype(BF16)


def dot(a, b, dims=(((1,), (0,)), ((), ()))):
    return lax.dot_general(a, b, dims, preferred_element_type=F32)


def dot3(a, b, dims=(((1,), (0,)), ((), ()))):
    return dot(a[0], b[0], dims) + dot(a[0], b[1], dims) + dot(a[1], b[0], dims)


def panel_kernel(places, first, *refs):
    n = len(places)
    pieces, (factor, adj, w), refs = refs[:n], refs[n : n + 3], refs[n + 3 :]
    if not first:
        refs = refs[2:]
    out, sums, p_high, p_low, w_high, w_low = refs

    @pl.when(pl.program_id(0) == 0)
    def _():
        if first:
            sums[...] = jnp.zeros_like(sums)
        w_high[...], w_low[...] = two_terms(w[...])

    for piece, place in zip(pieces, places):
        high, low = two_terms(piece[...])
        for src, rows, dst in place:
            p_high[dst : dst + rows, :] = high[src : src + rows]
            p_low[dst : dst + rows, :] = low[src : src + rows]
    panel = p_high[...], p_low[...]
    sums[...] += dot3(panel, two_terms(factor[...]))
    out[...] = adj[...] - dot3(panel, (w_high[...], w_low[...]), (((0,), (0,)), ((), ())))


def panel_step(early, pieces, places, factor, adj, w, state, start, skip, size, tile):
    rows, cols = factor.shape
    depth = w.shape[0]
    at, off = start // tile, skip // tile
    held = pl.BlockSpec(memory_space=pltpu.VMEM)
    tiled = pl.BlockSpec((tile, cols), lambda i: (i + at, 0))
    n = len(early) + len(pieces)
    first = state is None
    args = [*early, *pieces, factor, adj, w]
    in_specs = [pl.BlockSpec((p.shape[0], tile), lambda i: (0, i + at)) for p in early]
    in_specs += [pl.BlockSpec((p.shape[0], tile), lambda i: (0, i + off)) for p in pieces] + [tiled, tiled, held]
    aliases = {}
    if not first:
        args += [state[1], state[0]]
        in_specs += [held, pl.BlockSpec(memory_space=pl.ANY)]
        aliases = {n + 3: 1, n + 4: 0}
    return pl.pallas_call(
        functools.partial(panel_kernel, places, first),
        grid=(size // tile,),
        in_specs=in_specs,
        out_specs=[tiled, held],
        out_shape=[jax.ShapeDtypeStruct((rows, cols), F32), pltpu.VMEM((depth, cols), F32)],
        input_output_aliases=aliases,
        scratch_shapes=[pltpu.VMEM((depth, tile), BF16)] * 2 + [pltpu.VMEM((depth, cols), BF16)] * 2,
        compiler_params=pltpu.CompilerParams(vmem_limit_bytes=VMEM_BYTES),
        cost_estimate=pl.CostEstimate(
            flops=18 * size * depth * cols, bytes_accessed=12 * size * cols, transcendentals=0
        ),
    )(*args)


def cut(rows):
    tile = 256
    while rows % tile or rows // tile < 14:
        tile //= 2
    tiles = rows // tile
    part = tiles // 14
    sizes = [part, 4 * part, 4 * part, tiles - 11 * part, 2 * part]
    return [s * tile for s in sizes], tile


def after(x, *done):
    return lax.optimization_barrier((x, *done))[0] if done else x


def local(panel_adj, inv_diag, row_panel, trailing_adj, trailing_factor):
    n_row, n_col = lax.axis_size("row"), lax.axis_size("col")
    rows, kb = panel_adj.shape
    depth = kb * n_col
    planes = n_col // 4
    pairs = dict(
        x=[(c, c ^ 1) for c in range(n_col)],
        y=[(c, c ^ 2) for c in range(n_col)],
        up=[(c, (c + 4) % n_col) for c in range(n_col)],
        down=[(c, (c - 4) % n_col) for c in range(n_col)],
    )

    def send(way, x, *done):
        return lax.ppermute(after(x, *done), "col", pairs[way])

    def over_row(x, *done):
        if n_row == 2:
            return x + lax.ppermute(after(x, *done), "row", [(0, 1), (1, 0)])
        return lax.psum(x, "row")

    def cross(block, *done):
        block = after(block, *done)
        return send("x", block), send("y", block)

    def corner(x, y, *done):
        x, y = lax.optimization_barrier((x, y, *done))[:2]
        half = x.shape[0] // 2
        return send("x", y[:half]), send("y", x[half:])

    def along_z(block, *done):
        block = after(block, *done)
        return [block] + [
            lax.ppermute(block, "col", [(c, (c + 4 * j) % n_col) for c in range(n_col)]) for j in range(1, planes)
        ]

    own = panel_adj.T
    share = depth // n_row
    inv_own = lax.dynamic_slice(inv_diag, (0, lax.axis_index("row") * share), (kb, share))
    sizes, tile = cut(rows)
    starts = [sum(sizes[:i]) for i in range(len(sizes))]
    chunk = [own[:, a : a + n] for a, n in zip(starts, sizes)]
    n1 = sizes[0]
    chunk[0] = jnp.concatenate([chunk[0], inv_own], 1)
    wide1 = chunk[0].shape[1]

    def near(block, *done):
        return send("up", block, *done), send("down", block, *done)

    def far(block, up, down, *done):
        got = [block, up]
        while len(got) < planes - 1:
            got.append(send("up", got[-1], *done))
        return [*got, down]

    early = jnp.concatenate([chunk[0], chunk[4]], 1)
    z1 = along_z(chunk[0])
    x0, y0 = cross(early)
    xy0 = corner(x0, y0)
    z2 = along_z(chunk[1], x0, y0, *z1)
    rest1 = jnp.concatenate(z1[1:], 0)
    x1, y1 = cross(rest1, *xy0)
    d2 = jnp.concatenate(z2, 0)
    xy1 = corner(x1, y1)
    x2, y2 = cross(d2, x1, y1)
    z3 = along_z(chunk[2], *xy1)

    wide = kb * planes
    hk, hw, hr = kb // 2, wide // 2, (wide - kb) // 2
    z_places = [[(0, wide, 0)], [(0, wide, wide)], [(0, wide, 2 * wide)], [(0, hw, 3 * wide)], [(0, hw, 3 * wide + hw)]]
    p_places = [[(kb * q, kb, wide * q + kb * j) for q in range(4)] for j in range(planes)]
    first_places = [[(0, kb, 0)], [(0, kb, wide)], [(0, kb, 2 * wide)], [(0, hk, 3 * wide)], [(0, hk, 3 * wide + hk)],
                    [(0, wide - kb, kb)], [(0, wide - kb, wide + kb)], [(0, wide - kb, 2 * wide + kb)],
                    [(0, hr, 3 * wide + kb)], [(0, hr, 3 * wide + kb + hr)]]
    first = [p[:, :wide1] for p in (early, x0, y0, *xy0)] + [rest1, x1, y1, *xy1]
    inverse = jnp.concatenate([first[i][:, n1:] for i in (0, 5, 1, 6, 2, 7, 3, 4, 8, 9)], 0)
    w = over_row(jnp.dot(inverse, row_panel, precision=HIGH, preferred_element_type=F32))
    step = functools.partial(panel_step, [], factor=trailing_factor, adj=trailing_adj, w=w, tile=tile)

    def halves(got, state, c):
        size = sizes[c] // (2 * tile) * tile
        half = step(got, z_places, state=state, start=starts[c], skip=0, size=size)
        rest = sizes[c] - size
        return half, step(got, z_places, state=half, start=starts[c] + size, skip=size, size=rest)

    s1 = step(first, first_places, state=None, start=starts[0], skip=0, size=sizes[0])
    xy2 = corner(x2, y2, s1[1])
    d3 = jnp.concatenate(z3, 0)
    x3, y3 = cross(d3, x2, y2, s1[1])
    z4 = along_z(chunk[3], *xy2)
    s2a, s2 = halves([d2, x2, y2, *xy2], s1, 1)
    xy3 = corner(x3, y3, s2a[1])
    d4 = jnp.concatenate(z4, 0)
    x4, y4 = cross(d4, x3, y3, s2a[1])
    plane = jnp.concatenate([p[:, wide1:] for p in (early, x0, y0, *xy0)], 0)
    z5 = near(plane, z4[2], s2a[1])
    s3a, s3 = halves([d3, x3, y3, *xy3], s2, 2)
    xy4 = corner(x4, y4, s3a[1])
    z5 = far(plane, *z5)
    s5 = step(z5, p_places, state=s3, start=starts[4], skip=0, size=sizes[4])
    out, sums = step([d4, x4, y4, *xy4], z_places, state=s5, start=starts[3], skip=0, size=sizes[3])
    row_adj = lax.dot_general(
        inverse, over_row(sums), (((0,), (0,)), ((), ())), precision=HIGH, preferred_element_type=F32
    )
    return out, row_adj


def solution(mesh):
    placed = (P("row", "col"), P("col", None), P("row", "col"), P("row", "col"), P("row", "col"))
    return jax.shard_map(
        local,
        mesh=mesh,
        in_specs=placed,
        out_specs=(P("row", "col"), P("row", "col")),
        check_vma=False,
    )
```

```python
import functools

import jax
import jax.numpy as jnp
from jax import lax
from jax.experimental import pallas as pl
from jax.experimental.pallas import tpu as pltpu
from jax.sharding import PartitionSpec as P

F32, BF16 = jnp.float32, jnp.bfloat16
VMEM_BYTES = 32 << 20
HIGH = lax.Precision.HIGH


def two_terms(x):
    high = x.astype(BF16)
    return high, (x - high.astype(F32)).astype(BF16)


def dot(a, b, dims=(((1,), (0,)), ((), ()))):
    return lax.dot_general(a, b, dims, preferred_element_type=F32)


def dot3(a, b, dims=(((1,), (0,)), ((), ()))):
    return dot(a[0], b[0], dims) + dot(a[0], b[1], dims) + dot(a[1], b[0], dims)


def panel_kernel(places, first, *refs):
    n = len(places)
    pieces, (factor, adj, w), refs = refs[:n], refs[n : n + 3], refs[n + 3 :]
    if not first:
        refs = refs[2:]
    out, sums, p_high, p_low, w_high, w_low = refs

    @pl.when(pl.program_id(0) == 0)
    def _():
        if first:
            sums[...] = jnp.zeros_like(sums)
        w_high[...], w_low[...] = two_terms(w[...])

    for piece, place in zip(pieces, places):
        high, low = two_terms(piece[...])
        for src, rows, dst in place:
            p_high[dst : dst + rows, :] = high[src : src + rows]
            p_low[dst : dst + rows, :] = low[src : src + rows]
    panel = p_high[...], p_low[...]
    sums[...] += dot3(panel, two_terms(factor[...]))
    out[...] = adj[...] - dot3(panel, (w_high[...], w_low[...]), (((0,), (0,)), ((), ())))


def panel_step(early, pieces, places, factor, adj, w, state, start, skip, size, tile):
    rows, cols = factor.shape
    depth = w.shape[0]
    at, off = start // tile, skip // tile
    held = pl.BlockSpec(memory_space=pltpu.VMEM)
    tiled = pl.BlockSpec((tile, cols), lambda i: (i + at, 0))
    n = len(early) + len(pieces)
    first = state is None
    args = [*early, *pieces, factor, adj, w]
    in_specs = [pl.BlockSpec((p.shape[0], tile), lambda i: (0, i + at)) for p in early]
    in_specs += [pl.BlockSpec((p.shape[0], tile), lambda i: (0, i + off)) for p in pieces] + [tiled, tiled, held]
    aliases = {}
    if not first:
        args += [state[1], state[0]]
        in_specs += [held, pl.BlockSpec(memory_space=pl.ANY)]
        aliases = {n + 3: 1, n + 4: 0}
    return pl.pallas_call(
        functools.partial(panel_kernel, places, first),
        grid=(size // tile,),
        in_specs=in_specs,
        out_specs=[tiled, held],
        out_shape=[jax.ShapeDtypeStruct((rows, cols), F32), pltpu.VMEM((depth, cols), F32)],
        input_output_aliases=aliases,
        scratch_shapes=[pltpu.VMEM((depth, tile), BF16)] * 2 + [pltpu.VMEM((depth, cols), BF16)] * 2,
        compiler_params=pltpu.CompilerParams(vmem_limit_bytes=VMEM_BYTES),
        cost_estimate=pl.CostEstimate(
            flops=18 * size * depth * cols, bytes_accessed=12 * size * cols, transcendentals=0
        ),
    )(*args)


def cut(rows):
    tile = 256
    while rows % tile or rows // tile < 14:
        tile //= 2
    tiles = rows // tile
    part = tiles // 14
    sizes = [part, 4 * part, 4 * part, tiles - 11 * part, 2 * part]
    return [s * tile for s in sizes], tile


def after(x, *done):
    return lax.optimization_barrier((x, *done))[0] if done else x


def local(panel_adj, inv_diag, row_panel, trailing_adj, trailing_factor):
    n_row, n_col = lax.axis_size("row"), lax.axis_size("col")
    rows, kb = panel_adj.shape
    depth = kb * n_col
    planes = n_col // 4
    pairs = dict(
        x=[(c, c ^ 1) for c in range(n_col)],
        y=[(c, c ^ 2) for c in range(n_col)],
        up=[(c, (c + 4) % n_col) for c in range(n_col)],
        down=[(c, (c - 4) % n_col) for c in range(n_col)],
    )

    def send(way, x, *done):
        return lax.ppermute(after(x, *done), "col", pairs[way])

    def over_row(x, *done):
        if n_row == 2:
            return x + lax.ppermute(after(x, *done), "row", [(0, 1), (1, 0)])
        return lax.psum(x, "row")

    def cross(block, *done):
        block = after(block, *done)
        return send("x", block), send("y", block)

    def corner(x, y, *done):
        x, y = lax.optimization_barrier((x, y, *done))[:2]
        half = x.shape[0] // 2
        return send("x", y[:half]), send("y", x[half:])

    def along_z(block, *done):
        block = after(block, *done)
        return [block] + [
            lax.ppermute(block, "col", [(c, (c + 4 * j) % n_col) for c in range(n_col)]) for j in range(1, planes)
        ]

    own = panel_adj.T
    share = depth // n_row
    inv_own = lax.dynamic_slice(inv_diag, (0, lax.axis_index("row") * share), (kb, share))
    sizes, tile = cut(rows)
    starts = [sum(sizes[:i]) for i in range(len(sizes))]
    chunk = [own[:, a : a + n] for a, n in zip(starts, sizes)]
    n1 = sizes[0]
    chunk[0] = jnp.concatenate([chunk[0], inv_own], 1)
    wide1 = chunk[0].shape[1]

    def near(block, *done):
        return send("up", block, *done), send("down", block, *done)

    def far(block, up, down, *done):
        got = [block, up]
        while len(got) < planes - 1:
            got.append(send("up", got[-1], *done))
        return [*got, down]

    early = jnp.concatenate([chunk[0], chunk[4]], 1)
    z1 = along_z(chunk[0])
    x0, y0 = cross(early)
    xy0 = corner(x0, y0)
    z2 = along_z(chunk[1], x0, y0, *z1)
    rest1 = jnp.concatenate(z1[1:], 0)
    x1, y1 = cross(rest1, *xy0)
    d2 = jnp.concatenate(z2, 0)
    xy1 = corner(x1, y1)
    x2, y2 = cross(d2, x1, y1)
    z3 = along_z(chunk[2], *xy1)

    wide = kb * planes
    hk, hw, hr = kb // 2, wide // 2, (wide - kb) // 2
    z_places = [[(0, wide, 0)], [(0, wide, wide)], [(0, wide, 2 * wide)], [(0, hw, 3 * wide)], [(0, hw, 3 * wide + hw)]]
    p_places = [[(kb * q, kb, wide * q + kb * j) for q in range(4)] for j in range(planes)]
    first_places = [[(0, kb, 0)], [(0, kb, wide)], [(0, kb, 2 * wide)], [(0, hk, 3 * wide)], [(0, hk, 3 * wide + hk)],
                    [(0, wide - kb, kb)], [(0, wide - kb, wide + kb)], [(0, wide - kb, 2 * wide + kb)],
                    [(0, hr, 3 * wide + kb)], [(0, hr, 3 * wide + kb + hr)]]
    first = [p[:, :wide1] for p in (early, x0, y0, *xy0)] + [rest1, x1, y1, *xy1]
    inverse = jnp.concatenate([first[i][:, n1:] for i in (0, 5, 1, 6, 2, 7, 3, 4, 8, 9)], 0)
    w = over_row(jnp.dot(inverse, row_panel, precision=HIGH, preferred_element_type=F32))
    step = functools.partial(panel_step, [], factor=trailing_factor, adj=trailing_adj, w=w, tile=tile)

    def halves(got, state, c):
        size = sizes[c] // (2 * tile) * tile
        half = step(got, z_places, state=state, start=starts[c], skip=0, size=size)
        rest = sizes[c] - size
        return half, step(got, z_places, state=half, start=starts[c] + size, skip=size, size=rest)

    s1 = step(first, first_places, state=None, start=starts[0], skip=0, size=sizes[0])
    xy2 = corner(x2, y2, s1[1])
    d3 = jnp.concatenate(z3, 0)
    x3, y3 = cross(d3, x2, y2, s1[1])
    z4 = along_z(chunk[3], *xy2)
    s2a, s2 = halves([d2, x2, y2, *xy2], s1, 1)
    xy3 = corner(x3, y3, s2a[1])
    d4 = jnp.concatenate(z4, 0)
    x4, y4 = cross(d4, x3, y3, s2a[1])
    plane = jnp.concatenate([p[:, wide1:] for p in (early, x0, y0, *xy0)], 0)
    z5 = near(plane, z4[2])
    s3a, s3 = halves([d3, x3, y3, *xy3], s2, 2)
    xy4 = corner(x4, y4, s3a[1])
    z5 = far(plane, *z5)
    s5 = step(z5, p_places, state=s3, start=starts[4], skip=0, size=sizes[4])
    out, sums = step([d4, x4, y4, *xy4], z_places, state=s5, start=starts[3], skip=0, size=sizes[3])
    row_adj = lax.dot_general(
        inverse, over_row(sums), (((0,), (0,)), ((), ())), precision=HIGH, preferred_element_type=F32
    )
    return out, row_adj


def solution(mesh):
    placed = (P("row", "col"), P("col", None), P("row", "col"), P("row", "col"), P("row", "col"))
    return jax.shard_map(
        local,
        mesh=mesh,
        in_specs=placed,
        out_specs=(P("row", "col"), P("row", "col")),
        check_vma=False,
    )
```
